32 devices in a mesh: seq: 32 (over z, y, x, core), chan: 1.
Axes of the slice: x: 2, y: 2, z: 4, core: 2. Of those that a mesh axis runs over, the one named last changes fastest.
Arguments:
- tokens: bfloat16 [1536, 16384], P('chan', 'seq'), may hold values from -6 to 6
- gate_weight: bfloat16 [1536, 1536], P('chan'), may hold values from -0.15625 to 0.15625
- value_weight: bfloat16 [1536, 1536], P('chan'), may hold values from -0.15625 to 0.15625
- first_factor: bfloat16 [64, 256, 256], P('seq'), may hold values from -0.375 to 0.375
- second_factor: bfloat16 [256, 64, 64], P('seq'), may hold values from -0.75 to 0.75
- down_latent: bfloat16 [1536, 128], P('chan'), may hold values from -0.15625 to 0.15625
- up_latent: bfloat16 [1536, 128], P('chan'), may hold values from -0.5 to 0.5
- doc_lengths: int32 [64], replicated, may hold values from 1 to 8704, 16384 in all
- cotangent: bfloat16 [1536, 16384], P('chan', 'seq'), may hold values from -6 to 6
Outputs:
- hidden: bfloat16 [1536, 16384], P('chan', 'seq')
- d_gate_weight: float32 [1536, 1536], P('chan')
- d_value_weight: float32 [1536, 1536], P('chan')
- d_first: float32 [64, 256, 256], P('seq', 'chan')
- d_second: float32 [256, 64, 64], P('seq', 'chan')
- d_down: float32 [1536, 128], P('chan')
- d_up: float32 [1536, 128], P('chan')
The draws below stay inside these ranges and needn't reach their ends.
Inputs may be any that keep to these rules, and one draw needn't show every extreme that they name: `doc_lengths`: the documents' lengths sum to 16384; the longest is exactly 8704 tokens.
All inputs are finite; a program needn't handle non-finite values.
Results may differ from the reference program's by a relative error of at most 0.0058.
Values may be sent and summed in bfloat16 or wider, within the bound.
A program may use at most 128 MiB of HBM per device.

```python
import math
import jax
import jax.numpy as jnp
import numpy as np
from jax import lax

D = 1536
BLK = 256
LAT = 128
TOKENS = 16384
NB1 = 64
NDOC = 64
MOST = 8704


def shard_levels(rng, extent, shards, least, top_value):
    loudness, own = 1.0, jax.random.fold_in(rng, 6)
    for axis_at, blocks in shards:
        heights = jnp.exp(jax.random.uniform(jax.random.fold_in(own, axis_at), (blocks,), jnp.float32, least / len(shards), top_value / len(shards)))
        loudness = loudness * jnp.repeat(heights, extent[axis_at] // blocks).reshape([-1 if axis == axis_at else 1 for axis in range(len(extent))])
    return loudness


def profile(number_of, total, reach, slope):
    weights = [(1 << 20) // math.isqrt(grade ** slope) + 1 for grade in range(2, number_of + 1)]
    spare, given = total - reach - (number_of - 1), [1] * (number_of - 1)
    while spare > 0:
        free = [i for i in range(number_of - 1) if given[i] < reach]
        whole, left = sum([weights[i] for i in free]), spare
        for i in free:
            addition = min(reach - given[i], max(1, left * weights[i] // whole), spare)
            given[i] = given[i] + addition
            spare = spare - addition
    return np.array([reach] + given)


def ragged_sizes(own_key, amount, total, bound, lean):
    if amount == 2:
        one = jax.random.randint(own_key, (), max(1, total - bound), min(bound, total - 1) + 1)
        return jnp.stack([one, total - one])
    lengths = jnp.asarray(profile(amount, total, bound, lean), jnp.int32)
    twos = (amount - 1) // 2
    donor, sink = lengths[1:1 + 2 * twos:2], lengths[2:2 + 2 * twos:2]
    room = jnp.minimum(donor - 1, bound - sink)
    passed = jax.random.randint(jax.random.fold_in(own_key, 1), (twos,), 0, 1 << 20) % (room + 1)
    lengths = lengths.at[1:1 + 2 * twos:2].set(donor - passed).at[2:2 + 2 * twos:2].set(sink + passed)
    return lengths[jax.random.permutation(jax.random.fold_in(own_key, 2), amount)]


def noise(rng, shape, deviation, limit, cuts=(), kind=jnp.bfloat16):
    result = deviation * jax.random.normal(rng, shape, jnp.float32)
    if cuts:
        result = result * shard_levels(rng, shape, cuts, -0.22, 0.18)
    return jnp.clip(result, -limit, limit).astype(kind)


def setup_inputs(seed: int = 0) -> dict:
    key_list = jax.random.split(jax.random.key(seed), 10)
    tokens = noise(key_list[0], (D, TOKENS), 1.0, 6.0, ((1, 32),))
    gate_weight = noise(key_list[1], (D, D), D ** -0.5, 0.15625)
    value_weight = noise(key_list[2], (D, D), D ** -0.5, 0.15625)
    first_factor = noise(key_list[3], (NB1, BLK, BLK), BLK ** -0.5, 0.375, ((0, 32),))
    second_factor = noise(key_list[4], (BLK, NB1, NB1), NB1 ** -0.5, 0.75, ((0, 32),))
    down_latent = noise(key_list[5], (D, LAT), D ** -0.5, 0.15625)
    up_latent = noise(key_list[6], (D, LAT), LAT ** -0.5, 0.5)
    doc_lengths = ragged_sizes(key_list[7], NDOC, TOKENS, MOST, 2).astype(jnp.int32)
    cotangent = noise(key_list[8], (D, TOKENS), 1.0, 6.0, ((1, 32),))
    return {"tokens": tokens, "gate_weight": gate_weight, "value_weight": value_weight, "first_factor": first_factor, "second_factor": second_factor, "down_latent": down_latent, "up_latent": up_latent, "doc_lengths": doc_lengths, "cotangent": cotangent}


def reference(tokens, gate_weight, value_weight, first_factor, second_factor, down_latent, up_latent, doc_lengths, cotangent):
    highest = lax.Precision.HIGHEST
    inputs = tokens.T
    gate_w = gate_weight.T
    value_w = value_weight.T
    up_w = up_latent.T
    gate_pre = jnp.dot(inputs, gate_w, preferred_element_type=jnp.float32)
    value_bf = jnp.dot(inputs, value_w, preferred_element_type=jnp.float32).astype(jnp.bfloat16)
    doc_ends = jnp.cumsum(doc_lengths).astype(jnp.int32)
    doc_begins = (doc_ends - doc_lengths).astype(jnp.int32)
    position = jnp.arange(TOKENS, dtype=jnp.int32)
    member = ((position[:, None] >= doc_begins[None, :]) & (position[:, None] < doc_ends[None, :])).astype(jnp.float32)
    len_scale = lax.rsqrt(doc_lengths.astype(jnp.float32))
    latent = jnp.dot(inputs, down_latent, preferred_element_type=jnp.float32)
    pooled = jnp.dot(member.T, latent, precision=highest) * len_scale[:, None]
    spread = jnp.dot(pooled, up_w.astype(jnp.float32), precision=highest)
    summary = jnp.dot(member, spread, precision=highest)
    blocked = value_bf.reshape(NB1, BLK, D)
    inner_mix = jnp.einsum('ikj,ijc->ikc', first_factor.astype(jnp.float32), blocked.astype(jnp.float32)).astype(jnp.bfloat16)
    outer_mix = jnp.einsum('kmi,ikc->mkc', second_factor.astype(jnp.float32), inner_mix.astype(jnp.float32)).astype(jnp.bfloat16)
    mixed = outer_mix.reshape(TOKENS, D).astype(jnp.float32) + summary
    sig = jax.nn.sigmoid(gate_pre)
    act = gate_pre * sig
    hidden = (act * mixed).astype(jnp.bfloat16)
    upstream = cotangent.T.astype(jnp.float32)
    d_mixed = upstream * act
    d_mixed_bf = d_mixed.astype(jnp.bfloat16)
    d_gate_bf = (upstream * mixed * sig * (1.0 + gate_pre * (1.0 - sig))).astype(jnp.bfloat16)
    d_outer = d_mixed_bf.reshape(NB1, BLK, D).astype(jnp.float32)
    d_inner = jnp.einsum('kmi,mkc->ikc', second_factor.astype(jnp.float32), d_outer).astype(jnp.bfloat16)
    d_second = jnp.einsum('mkc,ikc->kmi', d_outer, inner_mix.astype(jnp.float32))
    d_value_bf = jnp.einsum('ikj,ikc->ijc', first_factor.astype(jnp.float32), d_inner.astype(jnp.float32)).astype(jnp.bfloat16).reshape(TOKENS, D)
    d_first = jnp.einsum('ikc,ijc->ikj', d_inner.astype(jnp.float32), blocked.astype(jnp.float32))
    per_doc = jnp.dot(member.T, d_mixed, precision=highest)
    d_up = jnp.dot(per_doc.T, pooled, precision=highest)
    d_pooled = jnp.dot(per_doc, up_w.astype(jnp.float32).T, precision=highest) * len_scale[:, None]
    d_latent_bf = jnp.dot(member, d_pooled, precision=highest).astype(jnp.bfloat16)
    d_down = jnp.dot(inputs.T, d_latent_bf, preferred_element_type=jnp.float32)
    d_gate_weight = jnp.dot(d_gate_bf.T, inputs, preferred_element_type=jnp.float32)
    d_value_weight = jnp.dot(d_value_bf.T, inputs, preferred_element_type=jnp.float32)
    return (hidden.T, d_gate_weight, d_value_weight, d_first, d_second, d_down, d_up)
```

```python
import functools

import jax
import jax.numpy as jnp
from jax import lax
from jax.sharding import PartitionSpec as P


def body(
    tokens,
    gate_weight,
    value_weight,
    first_factor,
    second_factor,
    down_latent,
    up_latent,
    doc_lengths,
    cotangent,
):
    highest = lax.Precision.HIGHEST
    chan_rows, tok_cols = tokens.shape
    block_width = first_factor.shape[1]
    blocks_here = tok_cols // block_width
    gathered = lax.all_gather(tokens, "chan", axis=0, tiled=True)
    gate_pre = jnp.dot(gate_weight, gathered, preferred_element_type=jnp.float32)
    value_acc = jnp.dot(value_weight, gathered, preferred_element_type=jnp.float32)
    value_bf = value_acc.astype(jnp.bfloat16)
    doc_ends = jnp.cumsum(doc_lengths)
    doc_begins = doc_ends - doc_lengths
    position = lax.axis_index("seq") * tok_cols + jnp.arange(tok_cols, dtype=jnp.int32)
    member = (
        (position[None, :] >= doc_begins[:, None]) & (position[None, :] < doc_ends[:, None])
    ).astype(jnp.float32)
    len_scale = lax.rsqrt(doc_lengths.astype(jnp.float32))
    latent_part = jnp.einsum("ct,cl->lt", tokens, down_latent, preferred_element_type=jnp.float32)
    latent_full = lax.psum(latent_part, "chan")
    doc_sums = lax.psum(jnp.einsum("dt,lt->dl", member, latent_full, precision=highest), "seq")
    pooled = doc_sums * len_scale[:, None]
    up_float = up_latent.astype(jnp.float32)
    spread_rows = jnp.einsum("cl,dl->cd", up_float, pooled, precision=highest)
    summary = jnp.dot(spread_rows, member, precision=highest)
    blocked = value_bf.reshape(chan_rows, blocks_here, block_width)
    inner_mix = jnp.einsum(
        "ikj,cij->kic", first_factor, blocked, preferred_element_type=jnp.float32
    ).astype(jnp.bfloat16)
    columns = lax.all_to_all(inner_mix, "seq", split_axis=0, concat_axis=1, tiled=True)
    outer_mix = jnp.einsum(
        "kmi,kic->kmc", second_factor, columns, preferred_element_type=jnp.float32
    ).astype(jnp.bfloat16)
    mixed_back = lax.all_to_all(outer_mix, "seq", split_axis=1, concat_axis=0, tiled=True)
    mixed = (
        jnp.transpose(mixed_back, (2, 1, 0)).reshape(chan_rows, tok_cols).astype(jnp.float32)
        + summary
    )
    sig = jax.nn.sigmoid(gate_pre)
    act = gate_pre * sig
    hidden = (act * mixed).astype(jnp.bfloat16)
    upstream = cotangent.astype(jnp.float32)
    d_mixed = upstream * act
    d_mixed_bf = d_mixed.astype(jnp.bfloat16)
    d_gate_bf = (upstream * mixed * sig * (1.0 + gate_pre * (1.0 - sig))).astype(jnp.bfloat16)
    d_send = jnp.transpose(d_mixed_bf.reshape(chan_rows, blocks_here, block_width), (2, 1, 0))
    d_outer = lax.all_to_all(d_send, "seq", split_axis=0, concat_axis=1, tiled=True)
    d_inner = jnp.einsum(
        "kmi,kmc->kic", second_factor, d_outer, preferred_element_type=jnp.float32
    ).astype(jnp.bfloat16)
    d_second_part = jnp.einsum("kmc,kic->kmi", d_outer, columns, preferred_element_type=jnp.float32)
    d_rows = lax.all_to_all(d_inner, "seq", split_axis=1, concat_axis=0, tiled=True)
    d_value_bf = (
        jnp.einsum("ikj,kic->cij", first_factor, d_rows, preferred_element_type=jnp.float32)
        .astype(jnp.bfloat16)
        .reshape(chan_rows, tok_cols)
    )
    d_first_part = jnp.einsum("kic,cij->ikj", d_rows, blocked, preferred_element_type=jnp.float32)
    per_doc = jnp.einsum("ct,dt->cd", d_mixed, member, precision=highest)
    d_up_part = jnp.einsum("cd,dl->cl", per_doc, pooled, precision=highest)
    d_pooled = lax.psum(
        jnp.einsum("cd,cl->dl", per_doc, up_float, precision=highest), ("seq", "chan")
    )
    d_latent_bf = jnp.einsum(
        "dl,dt->lt", d_pooled * len_scale[:, None], member, precision=highest
    ).astype(jnp.bfloat16)
    d_down_part = jnp.einsum("ct,lt->cl", tokens, d_latent_bf, preferred_element_type=jnp.float32)
    both_grads = jnp.concatenate([d_gate_bf, d_value_bf], axis=0)
    d_proj = jnp.einsum("ot,it->oi", both_grads, gathered, preferred_element_type=jnp.float32)
    d_proj, d_down, d_up = lax.psum((d_proj, d_down_part, d_up_part), "seq")
    d_first, d_second = (
        lax.psum_scatter(d_first_part, "chan", scatter_dimension=1, tiled=True),
        lax.psum_scatter(d_second_part, "chan", scatter_dimension=1, tiled=True),
    )
    return (hidden, d_proj[:chan_rows], d_proj[chan_rows:], d_first, d_second, d_down, d_up)


ROWS = 8


def swap(value, n, bit):
    pairs = [(i, i ^ (1 << bit)) for i in range(n)]
    return lax.ppermute(value, "seq", pairs)


def scatter_sum(part, n, bits, index):
    for bit in bits:
        half = part.shape[0] // 2
        mine = (index >> bit) & 1
        sent = lax.dynamic_slice_in_dim(part, (1 - mine) * half, half, 0)
        kept = lax.dynamic_slice_in_dim(part, mine * half, half, 0)
        got = swap(sent.astype(jnp.bfloat16), n, bit)
        part = kept + got.astype(jnp.float32)
    return part


def gather_all(piece, n, bits, index):
    for bit in reversed(bits):
        half = piece.shape[0]
        mine = (index >> bit) & 1
        got = swap(piece, n, bit)
        whole = jnp.zeros((2 * half,) + piece.shape[1:], piece.dtype)
        whole = lax.dynamic_update_slice_in_dim(whole, piece, mine * half, 0)
        piece = lax.dynamic_update_slice_in_dim(whole, got, (1 - mine) * half, 0)
    return piece


def streams_of(n):
    top = n.bit_length() - 1
    rest = list(range(1, top))
    orders = []
    for s in range(min(3, max(1, len(rest)))):
        if s == 0:
            order = rest
        elif s == 1:
            order = [rest[1], rest[0]] + rest[2:]
        else:
            order = rest[2:] + rest[:2]
        orders.append(order)
    return orders


def reduce_all(part, n, index):
    rows, cols = part.shape
    orders = streams_of(n)
    unit = n // 2
    low = 0
    blocks = part.reshape(2, rows // (2 * ROWS), ROWS, cols)
    mine = index & 1
    sent = lax.dynamic_index_in_dim(blocks, 1 - mine, 0, keepdims=False)
    kept = lax.dynamic_index_in_dim(blocks, mine, 0, keepdims=False)
    count = sent.shape[0] // unit
    shares = [(count * (s + 1)) // len(orders) - (count * s) // len(orders) for s in range(len(orders))]
    shares.sort(reverse=True)
    done = []
    for share, order in zip(shares, orders):
        if share == 0:
            continue
        at, size = low * unit, share * unit
        low += share
        got = swap(sent[at : at + size].astype(jnp.bfloat16), n, 0)
        piece = kept[at : at + size] + got.astype(jnp.float32)
        piece = scatter_sum(piece, n, order, index).astype(jnp.bfloat16)
        done.append((at, size, gather_all(piece, n, order, index)))
    ours = jnp.concatenate([piece for _, _, piece in done], axis=0)
    theirs = swap(ours, n, 0)
    first = jnp.where(mine == 0, ours, theirs)
    second = jnp.where(mine == 0, theirs, ours)
    return first, second


def seq_body(
    n,
    tokens,
    gate_weight,
    value_weight,
    first_factor,
    second_factor,
    down_latent,
    up_latent,
    doc_lengths,
    cotangent,
):
    highest = lax.Precision.HIGHEST
    f32, bf16 = jnp.float32, jnp.bfloat16
    width, count = tokens.shape
    here, block, _ = first_factor.shape
    share = second_factor.shape[0]
    index = lax.axis_index("seq")

    gate_pre = jnp.einsum("ct,oc->to", tokens, gate_weight, preferred_element_type=f32)
    sig = jax.nn.sigmoid(gate_pre)
    act = gate_pre * sig
    upstream = cotangent.T.astype(f32)
    d_mixed = upstream * act
    d_mixed_bf = d_mixed.astype(bf16)

    doc_ends = jnp.cumsum(doc_lengths)
    doc_begins = doc_ends - doc_lengths
    position = index * count + jnp.arange(count, dtype=jnp.int32)
    member = (
        (position[None, :] >= doc_begins[:, None]) & (position[None, :] < doc_ends[:, None])
    ).astype(f32)
    len_scale = lax.rsqrt(doc_lengths.astype(f32))
    up_float = up_latent.astype(f32)
    latent = jnp.einsum("ct,cl->tl", tokens, down_latent, preferred_element_type=f32)
    doc_part = jnp.dot(member, latent, precision=highest)
    per_doc = jnp.dot(member, d_mixed, precision=highest)
    d_pooled_part = jnp.dot(per_doc, up_float, precision=highest)
    small = jnp.concatenate([doc_part, d_pooled_part], axis=0)

    value_bf = jnp.einsum("ct,oc->to", tokens, value_weight, preferred_element_type=f32).astype(bf16)
    blocked = value_bf.reshape(here, block, width)
    inner_mix = jnp.einsum("ikj,ijc->ikc", first_factor, blocked, preferred_element_type=f32).astype(bf16)

    def outward(rows):
        rows = rows.reshape(here, n, share, width)
        return jnp.transpose(rows, (1, 0, 2, 3))

    def across(rows):
        return lax.all_to_all(rows, "seq", split_axis=0, concat_axis=0, tiled=True)

    inner_out = outward(inner_mix)
    inner_out, small = lax.optimization_barrier((inner_out, small))
    small = lax.psum(small, "seq")
    inner_k = across(inner_out).reshape(n * here, share, width)
    d_outer_k = across(outward(d_mixed_bf)).reshape(n * here, share, width)
    outer_k = jnp.einsum("kmi,ikc->mkc", second_factor, inner_k, preferred_element_type=f32).astype(bf16)
    outer_back = across(outer_k.reshape(n, here, share, width))
    d_inner_k = jnp.einsum("kmi,mkc->ikc", second_factor, d_outer_k, preferred_element_type=f32).astype(bf16)
    d_inner_back = across(d_inner_k.reshape(n, here, share, width))
    d_second = jnp.einsum("mkc,ikc->kmi", d_outer_k, inner_k, preferred_element_type=f32)

    docs = doc_part.shape[0]
    pooled = small[:docs] * len_scale[:, None]
    d_pooled = small[docs:] * len_scale[:, None]
    spread = jnp.dot(pooled, up_float.T, precision=highest)
    summary = jnp.einsum("dt,dc->tc", member, spread, precision=highest)
    mixed = jnp.transpose(outer_back, (1, 0, 2, 3)).reshape(count, width).astype(f32) + summary
    hidden = (act * mixed).astype(bf16).T
    d_gate_bf = (upstream * mixed * sig * (1.0 + gate_pre * (1.0 - sig))).astype(bf16)
    d_up_part = jnp.einsum("dl,dc->lc", pooled, per_doc, precision=highest)
    d_latent_bf = jnp.einsum("dl,dt->lt", d_pooled, member, precision=highest).astype(bf16)
    d_down_part = jnp.einsum("lt,ct->lc", d_latent_bf, tokens, preferred_element_type=f32)

    d_rows = jnp.transpose(d_inner_back, (1, 0, 2, 3)).reshape(here, block, width)
    d_value_bf = (
        jnp.einsum("ikj,ikc->ijc", first_factor, d_rows, preferred_element_type=f32)
        .astype(bf16)
        .reshape(count, width)
    )
    d_first = jnp.einsum("ikc,ijc->ikj", d_rows, blocked, preferred_element_type=f32)
    gate_part = jnp.einsum("to,it->oi", d_gate_bf, tokens, preferred_element_type=f32)
    value_part = jnp.einsum("to,it->oi", d_value_bf, tokens, preferred_element_type=f32)
    lats = d_up_part.shape[0]
    first, second = reduce_all(
        jnp.concatenate([gate_part, d_up_part, value_part, d_down_part], axis=0), n, index
    )
    first = first.reshape(-1, width)
    second = second.reshape(-1, width)
    return (
        hidden,
        first[:width].astype(f32),
        second[:width].astype(f32),
        d_first,
        d_second,
        second[width : width + lats].astype(f32).T,
        first[width : width + lats].astype(f32).T,
    )


def fits(n):
    return n >= 8 and n & (n - 1) == 0


def solution(mesh):
    n = mesh.shape["seq"]
    local = mesh.shape["chan"] == 1 and fits(n)
    run = functools.partial(seq_body, n) if local else body
    in_specs = (
        P("chan", "seq"),
        P("chan", None),
        P("chan", None),
        P("seq", None, None),
        P("seq", None, None),
        P("chan", None),
        P("chan", None),
        P(),
        P("chan", "seq"),
    )
    out_specs = (
        P("chan", "seq"),
        P("chan", None),
        P("chan", None),
        P("seq", "chan", None),
        P("seq", "chan", None),
        P("chan", None),
        P("chan", None),
    )
    return jax.shard_map(run, mesh=mesh, in_specs=in_specs, out_specs=out_specs, check_vma=False)
```

```python
import functools

import jax
import jax.numpy as jnp
from jax import lax
from jax.sharding import PartitionSpec as P


def body(
    tokens,
    gate_weight,
    value_weight,
    first_factor,
    second_factor,
    down_latent,
    up_latent,
    doc_lengths,
    cotangent,
):
    highest = lax.Precision.HIGHEST
    chan_rows, tok_cols = tokens.shape
    block_width = first_factor.shape[1]
    blocks_here = tok_cols // block_width
    gathered = lax.all_gather(tokens, "chan", axis=0, tiled=True)
    gate_pre = jnp.dot(gate_weight, gathered, preferred_element_type=jnp.float32)
    value_acc = jnp.dot(value_weight, gathered, preferred_element_type=jnp.float32)
    value_bf = value_acc.astype(jnp.bfloat16)
    doc_ends = jnp.cumsum(doc_lengths)
    doc_begins = doc_ends - doc_lengths
    position = lax.axis_index("seq") * tok_cols + jnp.arange(tok_cols, dtype=jnp.int32)
    member = (
        (position[None, :] >= doc_begins[:, None]) & (position[None, :] < doc_ends[:, None])
    ).astype(jnp.float32)
    len_scale = lax.rsqrt(doc_lengths.astype(jnp.float32))
    latent_part = jnp.einsum("ct,cl->lt", tokens, down_latent, preferred_element_type=jnp.float32)
    latent_full = lax.psum(latent_part, "chan")
    doc_sums = lax.psum(jnp.einsum("dt,lt->dl", member, latent_full, precision=highest), "seq")
    pooled = doc_sums * len_scale[:, None]
    up_float = up_latent.astype(jnp.float32)
    spread_rows = jnp.einsum("cl,dl->cd", up_float, pooled, precision=highest)
    summary = jnp.dot(spread_rows, member, precision=highest)
    blocked = value_bf.reshape(chan_rows, blocks_here, block_width)
    inner_mix = jnp.einsum(
        "ikj,cij->kic", first_factor, blocked, preferred_element_type=jnp.float32
    ).astype(jnp.bfloat16)
    columns = lax.all_to_all(inner_mix, "seq", split_axis=0, concat_axis=1, tiled=True)
    outer_mix = jnp.einsum(
        "kmi,kic->kmc", second_factor, columns, preferred_element_type=jnp.float32
    ).astype(jnp.bfloat16)
    mixed_back = lax.all_to_all(outer_mix, "seq", split_axis=1, concat_axis=0, tiled=True)
    mixed = (
        jnp.transpose(mixed_back, (2, 1, 0)).reshape(chan_rows, tok_cols).astype(jnp.float32)
        + summary
    )
    sig = jax.nn.sigmoid(gate_pre)
    act = gate_pre * sig
    hidden = (act * mixed).astype(jnp.bfloat16)
    upstream = cotangent.astype(jnp.float32)
    d_mixed = upstream * act
    d_mixed_bf = d_mixed.astype(jnp.bfloat16)
    d_gate_bf = (upstream * mixed * sig * (1.0 + gate_pre * (1.0 - sig))).astype(jnp.bfloat16)
    d_send = jnp.transpose(d_mixed_bf.reshape(chan_rows, blocks_here, block_width), (2, 1, 0))
    d_outer = lax.all_to_all(d_send, "seq", split_axis=0, concat_axis=1, tiled=True)
    d_inner = jnp.einsum(
        "kmi,kmc->kic", second_factor, d_outer, preferred_element_type=jnp.float32
    ).astype(jnp.bfloat16)
    d_second_part = jnp.einsum("kmc,kic->kmi", d_outer, columns, preferred_element_type=jnp.float32)
    d_rows = lax.all_to_all(d_inner, "seq", split_axis=1, concat_axis=0, tiled=True)
    d_value_bf = (
        jnp.einsum("ikj,kic->cij", first_factor, d_rows, preferred_element_type=jnp.float32)
        .astype(jnp.bfloat16)
        .reshape(chan_rows, tok_cols)
    )
    d_first_part = jnp.einsum("kic,cij->ikj", d_rows, blocked, preferred_element_type=jnp.float32)
    per_doc = jnp.einsum("ct,dt->cd", d_mixed, member, precision=highest)
    d_up_part = jnp.einsum("cd,dl->cl", per_doc, pooled, precision=highest)
    d_pooled = lax.psum(
        jnp.einsum("cd,cl->dl", per_doc, up_float, precision=highest), ("seq", "chan")
    )
    d_latent_bf = jnp.einsum(
        "dl,dt->lt", d_pooled * len_scale[:, None], member, precision=highest
    ).astype(jnp.bfloat16)
    d_down_part = jnp.einsum("ct,lt->cl", tokens, d_latent_bf, preferred_element_type=jnp.float32)
    both_grads = jnp.concatenate([d_gate_bf, d_value_bf], axis=0)
    d_proj = jnp.einsum("ot,it->oi", both_grads, gathered, preferred_element_type=jnp.float32)
    d_proj, d_down, d_up = lax.psum((d_proj, d_down_part, d_up_part), "seq")
    d_first, d_second = (
        lax.psum_scatter(d_first_part, "chan", scatter_dimension=1, tiled=True),
        lax.psum_scatter(d_second_part, "chan", scatter_dimension=1, tiled=True),
    )
    return (hidden, d_proj[:chan_rows], d_proj[chan_rows:], d_first, d_second, d_down, d_up)


ROWS = 8


def swap(value, n, bit):
    pairs = [(i, i ^ (1 << bit)) for i in range(n)]
    return lax.ppermute(value, "seq", pairs)


def streams_of(n):
    rest = list(range(1, n.bit_length() - 1))
    return [rest[s:] + rest[:s] for s in range(min(3, len(rest)))]


def reduce_all(part, n, index):
    rows, cols = part.shape
    orders = streams_of(n)
    unit = n // 2
    blocks = part.reshape(rows // ROWS, ROWS, cols)
    count = blocks.shape[0] // unit
    shares = [(count * (s + 1)) // len(orders) - (count * s) // len(orders) for s in range(len(orders))]
    shares.sort(reverse=True)
    pieces, low = [], 0
    for share in shares:
        pieces.append(blocks[low : low + share * unit])
        low += share * unit
    steps = len(orders[0])
    for step in range(steps):
        sent, kept = [], []
        for piece, order in zip(pieces, orders):
            half = piece.shape[0] // 2
            mine = (index >> order[step]) & 1
            sent.append(lax.dynamic_slice_in_dim(piece, (1 - mine) * half, half, 0).astype(jnp.bfloat16))
            kept.append(lax.dynamic_slice_in_dim(piece, mine * half, half, 0))
        sent = lax.optimization_barrier(tuple(sent))
        got = [swap(value, n, order[step]) for value, order in zip(sent, orders)]
        got = lax.optimization_barrier(tuple(got))
        pieces = [k + g.astype(jnp.float32) for k, g in zip(kept, got)]
    pieces = [piece.astype(jnp.bfloat16) for piece in pieces]
    for step in reversed(range(steps)):
        pieces = lax.optimization_barrier(tuple(pieces))
        got = [swap(value, n, order[step]) for value, order in zip(pieces, orders)]
        got = lax.optimization_barrier(tuple(got))
        joined = []
        for piece, other, order in zip(pieces, got, orders):
            half = piece.shape[0]
            mine = (index >> order[step]) & 1
            whole = jnp.zeros((2 * half,) + piece.shape[1:], piece.dtype)
            whole = lax.dynamic_update_slice_in_dim(whole, piece, mine * half, 0)
            joined.append(lax.dynamic_update_slice_in_dim(whole, other, (1 - mine) * half, 0))
        pieces = joined
    return jnp.concatenate(pieces, axis=0)


def seq_body(
    n,
    tokens,
    gate_weight,
    value_weight,
    first_factor,
    second_factor,
    down_latent,
    up_latent,
    doc_lengths,
    cotangent,
):
    highest = lax.Precision.HIGHEST
    f32, bf16 = jnp.float32, jnp.bfloat16
    width, count = tokens.shape
    here, block, _ = first_factor.shape
    lats = up_latent.shape[1]
    docs = doc_lengths.shape[0]
    share = second_factor.shape[0]
    index = lax.axis_index("seq")
    core = index & 1
    pair_tokens = jnp.concatenate([tokens, swap(tokens, n, 0)], axis=1)

    gate_pre = jnp.einsum("ct,oc->to", tokens, gate_weight, preferred_element_type=f32)
    sig = jax.nn.sigmoid(gate_pre)
    act = gate_pre * sig
    upstream = cotangent.T.astype(f32)
    d_mixed = upstream * act
    d_mixed_bf = d_mixed.astype(bf16)

    doc_ends = jnp.cumsum(doc_lengths)
    doc_begins = doc_ends - doc_lengths
    span = jnp.arange(count, dtype=jnp.int32)
    position = jnp.concatenate([index * count + span, (index ^ 1) * count + span])
    pair_member = (
        (position[None, :] >= doc_begins[:, None]) & (position[None, :] < doc_ends[:, None])
    ).astype(f32)
    member = pair_member[:, :count]
    len_scale = lax.rsqrt(doc_lengths.astype(f32))
    up_float = up_latent.astype(f32)
    latent = jnp.einsum("ct,cl->tl", tokens, down_latent, preferred_element_type=f32)
    doc_part = jnp.dot(member, latent, precision=highest)
    per_doc = jnp.dot(member, d_mixed, precision=highest)
    d_pooled_part = jnp.dot(per_doc, up_float, precision=highest)
    small = jnp.concatenate([doc_part, d_pooled_part], axis=0)

    value_bf = jnp.einsum("ct,oc->to", tokens, value_weight, preferred_element_type=f32).astype(bf16)
    blocked = value_bf.reshape(here, block, width)
    inner_mix = jnp.einsum("ikj,ijc->ikc", first_factor, blocked, preferred_element_type=f32).astype(bf16)

    def outward(rows):
        rows = rows.reshape(here, n, share, width)
        return jnp.transpose(rows, (1, 0, 2, 3))

    def across(rows):
        return lax.all_to_all(rows, "seq", split_axis=0, concat_axis=0, tiled=True)

    def half_columns(rows):
        half = rows.shape[1] // 2
        own = lax.dynamic_slice_in_dim(rows, core * half, half, 1)
        sent = lax.dynamic_slice_in_dim(rows, (1 - core) * half, half, 1)
        return jnp.concatenate([own, swap(sent, n, 0)], axis=0)

    def both_cores(blocks):
        theirs = swap(blocks, n, 0)
        place = lax.broadcasted_iota(jnp.int32, (2,) + blocks.shape, 0)
        return jnp.where(place == core, blocks[None], theirs[None])

    d_outer_out = outward(d_mixed_bf)
    d_outer_out, small, pair_per_doc, pair_tokens = lax.optimization_barrier(
        (d_outer_out, small, per_doc + swap(per_doc, n, 0), pair_tokens)
    )
    for bit in range(n.bit_length() - 1):
        small = small + swap(small, n, bit)
    pooled = small[:docs] * len_scale[:, None]
    d_pooled = small[docs:] * len_scale[:, None]

    d_outer_k = across(d_outer_out).reshape(n * here, share, width)
    d_inner_k = jnp.einsum("kmi,mkc->ikc", second_factor, d_outer_k, preferred_element_type=f32).astype(bf16)
    d_inner_k, inner_out = lax.optimization_barrier((d_inner_k, outward(inner_mix)))
    d_inner_back = across(d_inner_k.reshape(n, here, share, width))
    inner_out, d_inner_back = lax.optimization_barrier((inner_out, d_inner_back))
    inner_k = across(inner_out).reshape(n * here, share, width)

    d_rows = jnp.transpose(d_inner_back, (1, 0, 2, 3)).reshape(here, block, width)
    d_value_bf = (
        jnp.einsum("ikj,ikc->ijc", first_factor, d_rows, preferred_element_type=f32)
        .astype(bf16)
        .reshape(count, width)
    )
    half_lats = lats // 2
    our_pooled = lax.dynamic_slice_in_dim(pooled, core * half_lats, half_lats, 1)
    our_d_pooled = lax.dynamic_slice_in_dim(d_pooled, core * half_lats, half_lats, 1)
    d_up_part = jnp.einsum("dl,dc->lc", our_pooled, pair_per_doc, precision=highest)
    d_latent_bf = jnp.einsum("dl,dt->lt", our_d_pooled, pair_member, precision=highest).astype(bf16)
    d_down_part = jnp.einsum("lt,ct->lc", d_latent_bf, pair_tokens, preferred_element_type=f32)
    value_part = jnp.einsum(
        "to,it->oi", half_columns(d_value_bf), pair_tokens, preferred_element_type=f32
    )
    value_sum = both_cores(
        reduce_all(jnp.concatenate([value_part, d_up_part, d_down_part], axis=0), n, index)
    )

    outer_k = jnp.einsum("kmi,ikc->mkc", second_factor, inner_k, preferred_element_type=f32).astype(bf16)
    outer_back = across(outer_k.reshape(n, here, share, width))
    d_second = jnp.einsum("mkc,ikc->kmi", d_outer_k, inner_k, preferred_element_type=f32)
    d_first = jnp.einsum("ikc,ijc->ikj", d_rows, blocked, preferred_element_type=f32)

    spread = jnp.dot(pooled, up_float.T, precision=highest)
    summary = jnp.einsum("dt,dc->tc", member, spread, precision=highest)
    mixed = jnp.transpose(outer_back, (1, 0, 2, 3)).reshape(count, width).astype(f32) + summary
    d_gate_bf = (upstream * mixed * sig * (1.0 + gate_pre * (1.0 - sig))).astype(bf16)
    hidden = (act * mixed).astype(bf16).T
    gate_part = jnp.einsum(
        "to,it->oi", half_columns(d_gate_bf), pair_tokens, preferred_element_type=f32
    )
    gate_sum = both_cores(reduce_all(gate_part, n, index))

    blocks_w = width // 2 // ROWS
    blocks_l = half_lats // ROWS

    def rows_of(blocks, extent):
        return blocks.astype(f32).reshape(extent, width)

    return (
        hidden,
        rows_of(gate_sum, width),
        rows_of(value_sum[:, :blocks_w], width),
        d_first,
        d_second,
        rows_of(value_sum[:, blocks_w + blocks_l :], lats).T,
        rows_of(value_sum[:, blocks_w : blocks_w + blocks_l], lats).T,
    )


def fits(n):
    return n >= 8 and n & (n - 1) == 0


def solution(mesh):
    n = mesh.shape["seq"]
    local = mesh.shape["chan"] == 1 and fits(n)
    run = functools.partial(seq_body, n) if local else body
    in_specs = (
        P("chan", "seq"),
        P("chan", None),
        P("chan", None),
        P("seq", None, None),
        P("seq", None, None),
        P("chan", None),
        P("chan", None),
        P(),
        P("chan", "seq"),
    )
    out_specs = (
        P("chan", "seq"),
        P("chan", None),
        P("chan", None),
        P("seq", "chan", None),
        P("seq", "chan", None),
        P("chan", None),
        P("chan", None),
    )
    return jax.shard_map(run, mesh=mesh, in_specs=in_specs, out_specs=out_specs, check_vma=False)
```

```python
import functools

import jax
import jax.numpy as jnp
from jax import lax
from jax.sharding import PartitionSpec as P


def body(
    tokens,
    gate_weight,
    value_weight,
    first_factor,
    second_factor,
    down_latent,
    up_latent,
    doc_lengths,
    cotangent,
):
    highest = lax.Precision.HIGHEST
    chan_rows, tok_cols = tokens.shape
    block_width = first_factor.shape[1]
    blocks_here = tok_cols // block_width
    gathered = lax.all_gather(tokens, "chan", axis=0, tiled=True)
    gate_pre = jnp.dot(gate_weight, gathered, preferred_element_type=jnp.float32)
    value_acc = jnp.dot(value_weight, gathered, preferred_element_type=jnp.float32)
    value_bf = value_acc.astype(jnp.bfloat16)
    doc_ends = jnp.cumsum(doc_lengths)
    doc_begins = doc_ends - doc_lengths
    position = lax.axis_index("seq") * tok_cols + jnp.arange(tok_cols, dtype=jnp.int32)
    member = (
        (position[None, :] >= doc_begins[:, None]) & (position[None, :] < doc_ends[:, None])
    ).astype(jnp.float32)
    len_scale = lax.rsqrt(doc_lengths.astype(jnp.float32))
    latent_part = jnp.einsum("ct,cl->lt", tokens, down_latent, preferred_element_type=jnp.float32)
    latent_full = lax.psum(latent_part, "chan")
    doc_sums = lax.psum(jnp.einsum("dt,lt->dl", member, latent_full, precision=highest), "seq")
    pooled = doc_sums * len_scale[:, None]
    up_float = up_latent.astype(jnp.float32)
    spread_rows = jnp.einsum("cl,dl->cd", up_float, pooled, precision=highest)
    summary = jnp.dot(spread_rows, member, precision=highest)
    blocked = value_bf.reshape(chan_rows, blocks_here, block_width)
    inner_mix = jnp.einsum(
        "ikj,cij->kic", first_factor, blocked, preferred_element_type=jnp.float32
    ).astype(jnp.bfloat16)
    columns = lax.all_to_all(inner_mix, "seq", split_axis=0, concat_axis=1, tiled=True)
    outer_mix = jnp.einsum(
        "kmi,kic->kmc", second_factor, columns, preferred_element_type=jnp.float32
    ).astype(jnp.bfloat16)
    mixed_back = lax.all_to_all(outer_mix, "seq", split_axis=1, concat_axis=0, tiled=True)
    mixed = (
        jnp.transpose(mixed_back, (2, 1, 0)).reshape(chan_rows, tok_cols).astype(jnp.float32)
        + summary
    )
    sig = jax.nn.sigmoid(gate_pre)
    act = gate_pre * sig
    hidden = (act * mixed).astype(jnp.bfloat16)
    upstream = cotangent.astype(jnp.float32)
    d_mixed = upstream * act
    d_mixed_bf = d_mixed.astype(jnp.bfloat16)
    d_gate_bf = (upstream * mixed * sig * (1.0 + gate_pre * (1.0 - sig))).astype(jnp.bfloat16)
    d_send = jnp.transpose(d_mixed_bf.reshape(chan_rows, blocks_here, block_width), (2, 1, 0))
    d_outer = lax.all_to_all(d_send, "seq", split_axis=0, concat_axis=1, tiled=True)
    d_inner = jnp.einsum(
        "kmi,kmc->kic", second_factor, d_outer, preferred_element_type=jnp.float32
    ).astype(jnp.bfloat16)
    d_second_part = jnp.einsum("kmc,kic->kmi", d_outer, columns, preferred_element_type=jnp.float32)
    d_rows = lax.all_to_all(d_inner, "seq", split_axis=1, concat_axis=0, tiled=True)
    d_value_bf = (
        jnp.einsum("ikj,kic->cij", first_factor, d_rows, preferred_element_type=jnp.float32)
        .astype(jnp.bfloat16)
        .reshape(chan_rows, tok_cols)
    )
    d_first_part = jnp.einsum("kic,cij->ikj", d_rows, blocked, preferred_element_type=jnp.float32)
    per_doc = jnp.einsum("ct,dt->cd", d_mixed, member, precision=highest)
    d_up_part = jnp.einsum("cd,dl->cl", per_doc, pooled, precision=highest)
    d_pooled = lax.psum(
        jnp.einsum("cd,cl->dl", per_doc, up_float, precision=highest), ("seq", "chan")
    )
    d_latent_bf = jnp.einsum(
        "dl,dt->lt", d_pooled * len_scale[:, None], member, precision=highest
    ).astype(jnp.bfloat16)
    d_down_part = jnp.einsum("ct,lt->cl", tokens, d_latent_bf, preferred_element_type=jnp.float32)
    both_grads = jnp.concatenate([d_gate_bf, d_value_bf], axis=0)
    d_proj = jnp.einsum("ot,it->oi", both_grads, gathered, preferred_element_type=jnp.float32)
    d_proj, d_down, d_up = lax.psum((d_proj, d_down_part, d_up_part), "seq")
    d_first, d_second = (
        lax.psum_scatter(d_first_part, "chan", scatter_dimension=1, tiled=True),
        lax.psum_scatter(d_second_part, "chan", scatter_dimension=1, tiled=True),
    )
    return (hidden, d_proj[:chan_rows], d_proj[chan_rows:], d_first, d_second, d_down, d_up)


ROWS = 8


def swap(value, n, bit):
    pairs = [(i, i ^ (1 << bit)) for i in range(n)]
    return lax.ppermute(value, "seq", pairs)


def both(mine, other, place):
    where = lax.broadcasted_iota(jnp.int32, (2,) + mine.shape, 0)
    pair = jnp.where(where == place, mine[None], other[None])
    return pair.reshape((2 * mine.shape[0],) + mine.shape[1:])


def streams_of(n):
    rest = list(range(1, n.bit_length() - 1))
    return [rest[s:] + rest[:s] for s in range(min(3, len(rest)))]


def reduce_all(part, n, index, after=None):
    rows, cols = part.shape
    after = after or {}
    orders = streams_of(n)
    unit = n // 2
    blocks = part.reshape(rows // ROWS, ROWS, cols)
    count = blocks.shape[0] // unit
    shares = [(count * (s + 1)) // len(orders) - (count * s) // len(orders) for s in range(len(orders))]
    shares.sort(reverse=True)
    pieces, low = [], 0
    for share in shares:
        pieces.append(blocks[low : low + share * unit])
        low += share * unit
    steps = len(orders[0])
    for step in range(steps):
        sent, kept = [], []
        for piece, order in zip(pieces, orders):
            half = piece.shape[0] // 2
            mine = (index >> order[step]) & 1
            sent.append(lax.dynamic_slice_in_dim(piece, (1 - mine) * half, half, 0).astype(jnp.bfloat16))
            kept.append(lax.dynamic_slice_in_dim(piece, mine * half, half, 0))
        sent = lax.optimization_barrier(tuple(sent) + tuple(after.get(step, ())))[: len(sent)]
        got = [swap(value, n, order[step]) for value, order in zip(sent, orders)]
        got = lax.optimization_barrier(tuple(got))
        pieces = [k + g.astype(jnp.float32) for k, g in zip(kept, got)]
    pieces = [piece.astype(jnp.bfloat16) for piece in pieces]
    for step in reversed(range(steps)):
        pieces = lax.optimization_barrier(
            tuple(pieces) + tuple(after.get(2 * steps - 1 - step, ()))
        )[: len(pieces)]
        got = [swap(value, n, order[step]) for value, order in zip(pieces, orders)]
        got = lax.optimization_barrier(tuple(got))
        joined = []
        for piece, other, order in zip(pieces, got, orders):
            joined.append(both(piece, other, (index >> order[step]) & 1))
        pieces = joined
    return jnp.concatenate(pieces, axis=0)


def seq_body(
    n,
    tokens,
    gate_weight,
    value_weight,
    first_factor,
    second_factor,
    down_latent,
    up_latent,
    doc_lengths,
    cotangent,
):
    highest = lax.Precision.HIGHEST
    f32, bf16 = jnp.float32, jnp.bfloat16
    width, count = tokens.shape
    here, block, _ = first_factor.shape
    lats = up_latent.shape[1]
    docs = doc_lengths.shape[0]
    share = second_factor.shape[0]
    index = lax.axis_index("seq")
    core = index & 1
    pair_tokens = jnp.concatenate([tokens, swap(tokens, n, 0)], axis=1)

    gate_pre = jnp.einsum("ct,oc->to", tokens, gate_weight, preferred_element_type=f32)
    sig = jax.nn.sigmoid(gate_pre)
    act = gate_pre * sig
    upstream = cotangent.T.astype(f32)
    d_mixed = upstream * act
    d_mixed_bf = d_mixed.astype(bf16)

    doc_ends = jnp.cumsum(doc_lengths)
    doc_begins = doc_ends - doc_lengths
    span = jnp.arange(count, dtype=jnp.int32)
    position = jnp.concatenate([index * count + span, (index ^ 1) * count + span])
    pair_member = (
        (position[None, :] >= doc_begins[:, None]) & (position[None, :] < doc_ends[:, None])
    ).astype(f32)
    member = pair_member[:, :count]
    len_scale = lax.rsqrt(doc_lengths.astype(f32))
    up_float = up_latent.astype(f32)
    latent = jnp.einsum("ct,cl->tl", tokens, down_latent, preferred_element_type=f32)
    doc_part = jnp.dot(member, latent, precision=highest)
    per_doc = jnp.dot(member, d_mixed, precision=highest)
    d_pooled_part = jnp.dot(per_doc, up_float, precision=highest)
    small = jnp.concatenate([doc_part, d_pooled_part], axis=0)

    value_bf = jnp.einsum("ct,oc->to", tokens, value_weight, preferred_element_type=f32).astype(bf16)
    blocked = value_bf.reshape(here, block, width)
    inner_mix = jnp.einsum("ikj,ijc->ikc", first_factor, blocked, preferred_element_type=f32).astype(bf16)

    def outward(rows):
        rows = rows.reshape(here, n, share, width)
        return jnp.transpose(rows, (1, 0, 2, 3))

    def across(rows):
        return lax.all_to_all(rows, "seq", split_axis=0, concat_axis=0, tiled=True)

    def half_columns(rows):
        half = rows.shape[1] // 2
        own = lax.dynamic_slice_in_dim(rows, core * half, half, 1)
        sent = lax.dynamic_slice_in_dim(rows, (1 - core) * half, half, 1)
        return jnp.concatenate([own, swap(sent, n, 0)], axis=0)

    def both_cores(blocks):
        return both(blocks, swap(blocks, n, 0), core).reshape((2,) + blocks.shape)

    d_outer_out = outward(d_mixed_bf)
    d_outer_out, small, pair_per_doc, pair_tokens = lax.optimization_barrier(
        (d_outer_out, small, per_doc + swap(per_doc, n, 0), pair_tokens)
    )
    for bit in range(n.bit_length() - 1):
        small = small + swap(small, n, bit)
    pooled = small[:docs] * len_scale[:, None]
    d_pooled = small[docs:] * len_scale[:, None]

    same = jnp.eye(share, dtype=bf16)
    mixer = jnp.einsum("kmi,kq->mkiq", second_factor, same).reshape(n * here * share, n * here * share)
    mixer = mixer.astype(bf16)
    d_outer_rows = across(d_outer_out).reshape(n * here * share, width)
    d_outer_k = d_outer_rows.reshape(n * here, share, width)
    d_inner_k = jnp.einsum("pq,pc->qc", mixer, d_outer_rows, preferred_element_type=f32).astype(bf16)
    d_inner_k, inner_out = lax.optimization_barrier((d_inner_k, outward(inner_mix)))
    d_inner_back = across(d_inner_k.reshape(n, here, share, width))
    inner_out, d_inner_back = lax.optimization_barrier((inner_out, d_inner_back))
    inner_rows = across(inner_out).reshape(n * here * share, width)
    inner_k = inner_rows.reshape(n * here, share, width)

    d_rows = jnp.transpose(d_inner_back, (1, 0, 2, 3)).reshape(here, block, width)
    d_value_bf = (
        jnp.einsum("ikj,ikc->ijc", first_factor, d_rows, preferred_element_type=f32)
        .astype(bf16)
        .reshape(count, width)
    )
    half_lats = lats // 2
    our_pooled = lax.dynamic_slice_in_dim(pooled, core * half_lats, half_lats, 1)
    our_d_pooled = lax.dynamic_slice_in_dim(d_pooled, core * half_lats, half_lats, 1)
    d_up_part = jnp.einsum("dl,dc->lc", our_pooled, pair_per_doc, precision=highest)
    d_latent_bf = jnp.einsum("dl,dt->lt", our_d_pooled, pair_member, precision=highest).astype(bf16)
    d_down_part = jnp.einsum("lt,ct->lc", d_latent_bf, pair_tokens, preferred_element_type=f32)
    value_part = jnp.einsum(
        "to,it->oi", half_columns(d_value_bf), pair_tokens, preferred_element_type=f32
    )
    outer_k = jnp.einsum("pq,qc->pc", mixer, inner_rows, preferred_element_type=f32).astype(bf16)
    outer_back = across(outer_k.reshape(n, here, share, width))
    value_sum = both_cores(
        reduce_all(
            jnp.concatenate([value_part, d_up_part, d_down_part], axis=0),
            n,
            index,
            {2: (inner_rows,), 6: (outer_back,)},
        )
    )
    d_second = jnp.einsum("mkc,ikc->kmi", d_outer_k, inner_k, preferred_element_type=f32)
    d_first = jnp.einsum("ikc,ijc->ikj", d_rows, blocked, preferred_element_type=f32)

    spread = jnp.dot(pooled, up_float.T, precision=highest)
    summary = jnp.einsum("dt,dc->tc", member, spread, precision=highest)
    mixed = jnp.transpose(outer_back, (1, 0, 2, 3)).reshape(count, width).astype(f32) + summary
    d_gate_bf = (upstream * mixed * sig * (1.0 + gate_pre * (1.0 - sig))).astype(bf16)
    hidden = (act * mixed).astype(bf16).T
    gate_part = jnp.einsum(
        "to,it->oi", half_columns(d_gate_bf), pair_tokens, preferred_element_type=f32
    )
    gate_sum = both_cores(reduce_all(gate_part, n, index))

    blocks_w = width // 2 // ROWS
    blocks_l = half_lats // ROWS

    def rows_of(blocks, extent):
        return blocks.astype(f32).reshape(extent, width)

    return (
        hidden,
        rows_of(gate_sum, width),
        rows_of(value_sum[:, :blocks_w], width),
        d_first,
        d_second,
        rows_of(value_sum[:, blocks_w + blocks_l :], lats).T,
        rows_of(value_sum[:, blocks_w : blocks_w + blocks_l], lats).T,
    )


def fits(n):
    return n >= 8 and n & (n - 1) == 0


def solution(mesh):
    n = mesh.shape["seq"]
    local = mesh.shape["chan"] == 1 and fits(n)
    run = functools.partial(seq_body, n) if local else body
    in_specs = (
        P("chan", "seq"),
        P("chan", None),
        P("chan", None),
        P("seq", None, None),
        P("seq", None, None),
        P("chan", None),
        P("chan", None),
        P(),
        P("chan", "seq"),
    )
    out_specs = (
        P("chan", "seq"),
        P("chan", None),
        P("chan", None),
        P("seq", "chan", None),
        P("seq", "chan", None),
        P("chan", None),
        P("chan", None),
    )
    return jax.shard_map(run, mesh=mesh, in_specs=in_specs, out_specs=out_specs, check_vma=False)
```

```python
import functools

import jax
import jax.numpy as jnp
from jax import lax
from jax.sharding import PartitionSpec as P


def body(
    tokens,
    gate_weight,
    value_weight,
    first_factor,
    second_factor,
    down_latent,
    up_latent,
    doc_lengths,
    cotangent,
):
    highest = lax.Precision.HIGHEST
    chan_rows, tok_cols = tokens.shape
    block_width = first_factor.shape[1]
    blocks_here = tok_cols // block_width
    gathered = lax.all_gather(tokens, "chan", axis=0, tiled=True)
    gate_pre = jnp.dot(gate_weight, gathered, preferred_element_type=jnp.float32)
    value_acc = jnp.dot(value_weight, gathered, preferred_element_type=jnp.float32)
    value_bf = value_acc.astype(jnp.bfloat16)
    doc_ends = jnp.cumsum(doc_lengths)
    doc_begins = doc_ends - doc_lengths
    position = lax.axis_index("seq") * tok_cols + jnp.arange(tok_cols, dtype=jnp.int32)
    member = (
        (position[None, :] >= doc_begins[:, None]) & (position[None, :] < doc_ends[:, None])
    ).astype(jnp.float32)
    len_scale = lax.rsqrt(doc_lengths.astype(jnp.float32))
    latent_part = jnp.einsum("ct,cl->lt", tokens, down_latent, preferred_element_type=jnp.float32)
    latent_full = lax.psum(latent_part, "chan")
    doc_sums = lax.psum(jnp.einsum("dt,lt->dl", member, latent_full, precision=highest), "seq")
    pooled = doc_sums * len_scale[:, None]
    up_float = up_latent.astype(jnp.float32)
    spread_rows = jnp.einsum("cl,dl->cd", up_float, pooled, precision=highest)
    summary = jnp.dot(spread_rows, member, precision=highest)
    blocked = value_bf.reshape(chan_rows, blocks_here, block_width)
    inner_mix = jnp.einsum(
        "ikj,cij->kic", first_factor, blocked, preferred_element_type=jnp.float32
    ).astype(jnp.bfloat16)
    columns = lax.all_to_all(inner_mix, "seq", split_axis=0, concat_axis=1, tiled=True)
    outer_mix = jnp.einsum(
        "kmi,kic->kmc", second_factor, columns, preferred_element_type=jnp.float32
    ).astype(jnp.bfloat16)
    mixed_back = lax.all_to_all(outer_mix, "seq", split_axis=1, concat_axis=0, tiled=True)
    mixed = (
        jnp.transpose(mixed_back, (2, 1, 0)).reshape(chan_rows, tok_cols).astype(jnp.float32)
        + summary
    )
    sig = jax.nn.sigmoid(gate_pre)
    act = gate_pre * sig
    hidden = (act * mixed).astype(jnp.bfloat16)
    upstream = cotangent.astype(jnp.float32)
    d_mixed = upstream * act
    d_mixed_bf = d_mixed.astype(jnp.bfloat16)
    d_gate_bf = (upstream * mixed * sig * (1.0 + gate_pre * (1.0 - sig))).astype(jnp.bfloat16)
    d_send = jnp.transpose(d_mixed_bf.reshape(chan_rows, blocks_here, block_width), (2, 1, 0))
    d_outer = lax.all_to_all(d_send, "seq", split_axis=0, concat_axis=1, tiled=True)
    d_inner = jnp.einsum(
        "kmi,kmc->kic", second_factor, d_outer, preferred_element_type=jnp.float32
    ).astype(jnp.bfloat16)
    d_second_part = jnp.einsum("kmc,kic->kmi", d_outer, columns, preferred_element_type=jnp.float32)
    d_rows = lax.all_to_all(d_inner, "seq", split_axis=1, concat_axis=0, tiled=True)
    d_value_bf = (
        jnp.einsum("ikj,kic->cij", first_factor, d_rows, preferred_element_type=jnp.float32)
        .astype(jnp.bfloat16)
        .reshape(chan_rows, tok_cols)
    )
    d_first_part = jnp.einsum("kic,cij->ikj", d_rows, blocked, preferred_element_type=jnp.float32)
    per_doc = jnp.einsum("ct,dt->cd", d_mixed, member, precision=highest)
    d_up_part = jnp.einsum("cd,dl->cl", per_doc, pooled, precision=highest)
    d_pooled = lax.psum(
        jnp.einsum("cd,cl->dl", per_doc, up_float, precision=highest), ("seq", "chan")
    )
    d_latent_bf = jnp.einsum(
        "dl,dt->lt", d_pooled * len_scale[:, None], member, precision=highest
    ).astype(jnp.bfloat16)
    d_down_part = jnp.einsum("ct,lt->cl", tokens, d_latent_bf, preferred_element_type=jnp.float32)
    both_grads = jnp.concatenate([d_gate_bf, d_value_bf], axis=0)
    d_proj = jnp.einsum("ot,it->oi", both_grads, gathered, preferred_element_type=jnp.float32)
    d_proj, d_down, d_up = lax.psum((d_proj, d_down_part, d_up_part), "seq")
    d_first, d_second = (
        lax.psum_scatter(d_first_part, "chan", scatter_dimension=1, tiled=True),
        lax.psum_scatter(d_second_part, "chan", scatter_dimension=1, tiled=True),
    )
    return (hidden, d_proj[:chan_rows], d_proj[chan_rows:], d_first, d_second, d_down, d_up)


ROWS = 8


def swap(value, n, bit):
    pairs = [(i, i ^ (1 << bit)) for i in range(n)]
    return lax.ppermute(value, "seq", pairs)


def both(mine, other, place):
    where = lax.broadcasted_iota(jnp.int32, (2,) + mine.shape, 0)
    pair = jnp.where(where == place, mine[None], other[None])
    return pair.reshape((2 * mine.shape[0],) + mine.shape[1:])


def streams_of(n):
    rest = list(range(1, n.bit_length() - 1))
    return [rest[s:] + rest[:s] for s in range(min(3, len(rest)))]


def reduce_streams(part, n, index, after=None):
    rows, cols = part.shape
    after = after or {}
    orders = streams_of(n)
    unit = n // 2
    blocks = part.reshape(rows // ROWS, ROWS, cols)
    count = blocks.shape[0] // unit
    shares = [(count * (s + 1)) // len(orders) - (count * s) // len(orders) for s in range(len(orders))]
    shares.sort(reverse=True)
    pieces, low = [], 0
    for share in shares:
        pieces.append(blocks[low : low + share * unit])
        low += share * unit
    for step in range(len(orders[0])):
        sent, kept = [], []
        for piece, order in zip(pieces, orders):
            half = piece.shape[0] // 2
            mine = (index >> order[step]) & 1
            sent.append(lax.dynamic_slice_in_dim(piece, (1 - mine) * half, half, 0).astype(jnp.bfloat16))
            kept.append(lax.dynamic_slice_in_dim(piece, mine * half, half, 0))
        sent = lax.optimization_barrier(tuple(sent) + tuple(after.get(step, ())))[: len(sent)]
        got = [swap(value, n, order[step]) for value, order in zip(sent, orders)]
        got = lax.optimization_barrier(tuple(got))
        pieces = [k + g.astype(jnp.float32) for k, g in zip(kept, got)]
    return [piece.astype(jnp.bfloat16) for piece in pieces]


def gather_streams(firsts, seconds, n, index):
    orders = streams_of(n)
    cuts = [piece.shape[0] for piece in firsts]
    pieces = [jnp.concatenate([a, b], axis=0)[None] for a, b in zip(firsts, seconds)]
    for step in reversed(range(len(orders[0]))):
        pieces = lax.optimization_barrier(tuple(pieces))
        got = [swap(value, n, order[step]) for value, order in zip(pieces, orders)]
        got = lax.optimization_barrier(tuple(got))
        pieces = [
            both(piece, other, (index >> order[step]) & 1)
            for piece, other, order in zip(pieces, got, orders)
        ]

    def joined(parts):
        return jnp.concatenate([p.reshape((-1,) + p.shape[2:]) for p in parts], axis=0)

    return (
        joined([piece[:, :cut] for piece, cut in zip(pieces, cuts)]),
        joined([piece[:, cut:] for piece, cut in zip(pieces, cuts)]),
    )


def seq_body(
    n,
    tokens,
    gate_weight,
    value_weight,
    first_factor,
    second_factor,
    down_latent,
    up_latent,
    doc_lengths,
    cotangent,
):
    highest = lax.Precision.HIGHEST
    f32, bf16 = jnp.float32, jnp.bfloat16
    width, count = tokens.shape
    here, block, _ = first_factor.shape
    lats = up_latent.shape[1]
    docs = doc_lengths.shape[0]
    share = second_factor.shape[0]
    index = lax.axis_index("seq")
    core = index & 1
    pair_tokens = jnp.concatenate([tokens, swap(tokens, n, 0)], axis=1)

    gate_pre = jnp.einsum("ct,oc->to", tokens, gate_weight, preferred_element_type=f32)
    sig = jax.nn.sigmoid(gate_pre)
    act = gate_pre * sig
    upstream = cotangent.T.astype(f32)
    d_mixed = upstream * act
    d_mixed_bf = d_mixed.astype(bf16)

    doc_ends = jnp.cumsum(doc_lengths)
    doc_begins = doc_ends - doc_lengths
    span = jnp.arange(count, dtype=jnp.int32)
    position = jnp.concatenate([index * count + span, (index ^ 1) * count + span])
    pair_member = (
        (position[None, :] >= doc_begins[:, None]) & (position[None, :] < doc_ends[:, None])
    ).astype(f32)
    member = pair_member[:, :count]
    len_scale = lax.rsqrt(doc_lengths.astype(f32))
    up_float = up_latent.astype(f32)
    latent = jnp.einsum("ct,cl->tl", tokens, down_latent, preferred_element_type=f32)
    doc_part = jnp.dot(member, latent, precision=highest)
    per_doc = jnp.dot(member, d_mixed, precision=highest)
    d_pooled_part = jnp.dot(per_doc, up_float, precision=highest)
    small = jnp.concatenate([doc_part, d_pooled_part], axis=0)

    value_bf = jnp.einsum("ct,oc->to", tokens, value_weight, preferred_element_type=f32).astype(bf16)
    blocked = value_bf.reshape(here, block, width)
    inner_mix = jnp.einsum("ikj,ijc->ikc", first_factor, blocked, preferred_element_type=f32).astype(bf16)

    def outward(rows):
        rows = rows.reshape(here, n, share, width)
        return jnp.transpose(rows, (1, 0, 2, 3))

    def across(rows):
        return lax.all_to_all(rows, "seq", split_axis=0, concat_axis=0, tiled=True)

    def half_columns(rows):
        half = rows.shape[1] // 2
        own = lax.dynamic_slice_in_dim(rows, core * half, half, 1)
        sent = lax.dynamic_slice_in_dim(rows, (1 - core) * half, half, 1)
        return jnp.concatenate([own, swap(sent, n, 0)], axis=0)

    d_outer_out = outward(d_mixed_bf)
    d_outer_out, small, pair_per_doc, pair_tokens = lax.optimization_barrier(
        (d_outer_out, small, per_doc + swap(per_doc, n, 0), pair_tokens)
    )
    for bit in range(n.bit_length() - 1):
        small = small + swap(small, n, bit)
    pooled = small[:docs] * len_scale[:, None]
    d_pooled = small[docs:] * len_scale[:, None]

    same = jnp.eye(share, dtype=bf16)
    mixer = jnp.einsum("kmi,kq->mkiq", second_factor, same).reshape(n * here * share, n * here * share)
    mixer = mixer.astype(bf16)
    d_outer_rows = across(d_outer_out).reshape(n * here * share, width)
    d_outer_k = d_outer_rows.reshape(n * here, share, width)
    d_inner_k = jnp.einsum("pq,pc->qc", mixer, d_outer_rows, preferred_element_type=f32).astype(bf16)
    d_inner_k, inner_out = lax.optimization_barrier((d_inner_k, outward(inner_mix)))
    d_inner_back = across(d_inner_k.reshape(n, here, share, width))
    inner_out, d_inner_back = lax.optimization_barrier((inner_out, d_inner_back))
    inner_rows = across(inner_out).reshape(n * here * share, width)
    inner_k = inner_rows.reshape(n * here, share, width)

    d_rows = jnp.transpose(d_inner_back, (1, 0, 2, 3)).reshape(here, block, width)
    d_value_bf = (
        jnp.einsum("ikj,ikc->ijc", first_factor, d_rows, preferred_element_type=f32)
        .astype(bf16)
        .reshape(count, width)
    )
    half_lats = lats // 2
    our_pooled = lax.dynamic_slice_in_dim(pooled, core * half_lats, half_lats, 1)
    our_d_pooled = lax.dynamic_slice_in_dim(d_pooled, core * half_lats, half_lats, 1)
    d_up_part = jnp.einsum("dl,dc->lc", our_pooled, pair_per_doc, precision=highest)
    d_latent_bf = jnp.einsum("dl,dt->lt", our_d_pooled, pair_member, precision=highest).astype(bf16)
    d_down_part = jnp.einsum("lt,ct->lc", d_latent_bf, pair_tokens, preferred_element_type=f32)
    value_part = jnp.einsum(
        "to,it->oi", half_columns(d_value_bf), pair_tokens, preferred_element_type=f32
    )
    outer_k = jnp.einsum("pq,qc->pc", mixer, inner_rows, preferred_element_type=f32).astype(bf16)
    outer_back = across(outer_k.reshape(n, here, share, width))
    value_pieces = reduce_streams(
        jnp.concatenate([value_part, d_up_part, d_down_part], axis=0),
        n,
        index,
        {2: (inner_rows,)},
    )
    d_second = jnp.einsum("mkc,ikc->kmi", d_outer_k, inner_k, preferred_element_type=f32)
    d_first = jnp.einsum("ikc,ijc->ikj", d_rows, blocked, preferred_element_type=f32)

    spread = jnp.dot(pooled, up_float.T, precision=highest)
    summary = jnp.einsum("dt,dc->tc", member, spread, precision=highest)
    mixed = jnp.transpose(outer_back, (1, 0, 2, 3)).reshape(count, width).astype(f32) + summary
    d_gate_bf = (upstream * mixed * sig * (1.0 + gate_pre * (1.0 - sig))).astype(bf16)
    hidden = (act * mixed).astype(bf16).T
    gate_part = jnp.einsum(
        "to,it->oi", half_columns(d_gate_bf), pair_tokens, preferred_element_type=f32
    )
    gate_part, d_second, d_first, hidden = lax.optimization_barrier(
        (gate_part, d_second, d_first, hidden)
    )
    gate_pieces = reduce_streams(gate_part, n, index)
    value_ours, gate_ours = gather_streams(value_pieces, gate_pieces, n, index)
    value_ours, gate_ours = lax.optimization_barrier((value_ours, gate_ours))
    value_theirs, gate_theirs = lax.optimization_barrier(
        (swap(value_ours, n, 0), swap(gate_ours, n, 0))
    )
    blocks_w = width // 2 // ROWS
    blocks_l = half_lats // ROWS

    def rows_of(ours, theirs, low, size):
        rows = both(ours[low : low + size], theirs[low : low + size], core)
        return rows.astype(f32).reshape(2 * size * ROWS, width)

    return (
        hidden,
        rows_of(gate_ours, gate_theirs, 0, blocks_w),
        rows_of(value_ours, value_theirs, 0, blocks_w),
        d_first,
        d_second,
        rows_of(value_ours, value_theirs, blocks_w + blocks_l, blocks_l).T,
        rows_of(value_ours, value_theirs, blocks_w, blocks_l).T,
    )


def fits(n):
    return n >= 8 and n & (n - 1) == 0


def solution(mesh):
    n = mesh.shape["seq"]
    local = mesh.shape["chan"] == 1 and fits(n)
    run = functools.partial(seq_body, n) if local else body
    in_specs = (
        P("chan", "seq"),
        P("chan", None),
        P("chan", None),
        P("seq", None, None),
        P("seq", None, None),
        P("chan", None),
        P("chan", None),
        P(),
        P("chan", "seq"),
    )
    out_specs = (
        P("chan", "seq"),
        P("chan", None),
        P("chan", None),
        P("seq", "chan", None),
        P("seq", "chan", None),
        P("chan", None),
        P("chan", None),
    )
    return jax.shard_map(run, mesh=mesh, in_specs=in_specs, out_specs=out_specs, check_vma=False)
```
